32 devices in a mesh: groups: 2 (over x), dp: 16 (over z, y, core).
Axes of the slice: x: 2, y: 2, z: 4, core: 2. Of those that a mesh axis runs over, the one named last changes fastest.
Arguments:
- points: float32 [32, 32768], P(None, ('groups', 'dp')), parts along dimension 1, may hold values from -6 to 6
- centres: float32 [32, 8192], P(None, ('groups', 'dp')), parts along dimension 1, may hold values from -6 to 6
- direction: float32 [8192], P(('groups', 'dp')), parts along dimension 0, may hold values from -6 to 6
- counts: int32 [32], P(('groups', 'dp')), parts along dimension 0, may hold values from 256 to 1024, as said below
Outputs:
- product: float32 [8192], P(('groups', 'dp')), parts along dimension 0
The draws below stay inside these ranges and needn't reach their ends.
There are 2 independent parts, one for each index of `groups`. The reference program is written for one: setup_inputs(seed, part) draws one part's arguments, and reference() takes and returns one part's arrays. A program takes and returns all parts, laid end to end along the dimension named above; each array names one. Nothing has to cross between parts.
Inputs may be any that keep to these rules, and one draw needn't show every extreme that they name: `counts`: some index holds exactly 1024 live slots and some other exactly 256.
All inputs are finite; a program needn't handle non-finite values.
Results may differ from the reference program's by a relative error of at most 0.0003.
Values sent between devices are 32-bit elements; how exact they have to be, the bound alone decides.
A program may use at most 64 MiB of HBM per device.

```python
import jax
import jax.numpy as jnp
from jax import lax

D = 32
PTS_DEV = 1024
M = 4096
NTOT = 16384
N_DP = 16


def draw_counts(key, part):
    key = jax.random.fold_in(key, 7)
    first, second, third = jax.random.split(key, 3)
    values = jax.random.randint(first, (N_DP,), PTS_DEV // 4, PTS_DEV + 1)
    top = jax.random.randint(second, (), 0, N_DP)
    other = (top + 1 + jax.random.randint(third, (), 0, N_DP - 1)) % N_DP
    values = values.at[top].set(PTS_DEV)
    values = values.at[other].set(PTS_DEV // 4)
    return values.astype(jnp.int32)


def block_scale(key, shape, cuts, least, high):
    level = 1.0
    for axis_at, shards_of in cuts:
        draws = jax.random.uniform(jax.random.fold_in(jax.random.fold_in(key, 6), axis_at), (shards_of,), jnp.float32, least / len(cuts), high / len(cuts))
        level = level * jnp.repeat(jnp.exp(draws), shape[axis_at] // shards_of).reshape((-1,) + (1,) * (len(shape) - 1 - axis_at))
    return level


def bell_draw(rng, extent, scale, reach, cuts=(), kind=jnp.bfloat16):
    level = block_scale(rng, extent, cuts, -0.22, 0.18) if cuts else 1.0
    array = jax.random.normal(rng, extent, jnp.float32) * scale * level
    return jnp.minimum(jnp.maximum(array, -reach), reach).astype(kind)


def setup_inputs(seed: int = 0, part: int = 0) -> dict:
    keys = jax.random.split(jax.random.key(seed), 5)
    part_keys = jax.random.split(jax.random.fold_in(keys[4], part), 5)
    return {
        "points": bell_draw(part_keys[0], (D, NTOT), 1.0, 6.0, ((1, 16),), jnp.float32),
        "centres": bell_draw(part_keys[1], (D, M), 1.0, 6.0, ((1, 16),), jnp.float32),
        "direction": bell_draw(part_keys[2], (M,), 1.0, 6.0, ((0, 16),), jnp.float32),
        "counts": draw_counts(jax.random.fold_in(jax.random.fold_in(keys[4], part), 71), part),
    }


def kernel_rows(pts, cen, cen_norm):
    cross = lax.dot_general(pts, cen, (((0,), (0,)), ((), ())), precision=lax.Precision.HIGHEST, preferred_element_type=jnp.float32)
    pts_norm = lax.optimization_barrier(jnp.sum(pts * pts, axis=0))
    dist = pts_norm[:, None] + cen_norm[None, :] - 2.0 * cross
    return jnp.exp(-dist / pts.shape[0]).astype(jnp.bfloat16)

def reference(points, centres, direction, counts):
    width, total = points.shape
    count_m = centres.shape[1]
    blk = min(128, PTS_DEV)
    nblocks = total // blk
    cen_norm = lax.optimization_barrier(jnp.sum(centres * centres, axis=0))
    vdir = direction.astype(jnp.float32)
    blocks = points.reshape(width, nblocks, blk).transpose(1, 0, 2)
    slots = jnp.arange(total, dtype=jnp.int32).reshape(nblocks, blk)

    def step(acc, pair):
        pts, rows = pair
        kern = kernel_rows(pts, centres, cen_norm)
        live = rows % PTS_DEV < counts[rows // PTS_DEV]
        inner = jnp.dot(kern.astype(jnp.float32), vdir, precision=lax.Precision.HIGHEST, preferred_element_type=jnp.float32) / jnp.sqrt(jnp.float32(count_m))
        inner = jnp.where(live, inner, jnp.float32(0.0)).astype(jnp.bfloat16)
        return (acc + jnp.dot(inner, kern, preferred_element_type=jnp.float32), None)
    acc, _ = lax.scan(step, jnp.zeros((count_m,), jnp.float32), (blocks, slots))
    return acc / jnp.sqrt(jnp.float32(total))
```

```python
import functools
import math

import jax
import jax.numpy as jnp
from jax import lax
from jax.experimental import pallas as pl
from jax.experimental.pallas import tpu as pltpu
from jax.sharding import PartitionSpec as P

MESH = pl.DeviceIdType.MESH
KERN_BYTES = 16 << 20
F32, BF16 = jnp.float32, jnp.bfloat16


def split3(x):
    high = x.astype(BF16)
    rest = x - high.astype(F32)
    mid = rest.astype(BF16)
    low = (rest - mid.astype(F32)).astype(BF16)
    return high, mid, low


def rows_of(count, terms):
    columns = terms[0].shape[1]
    at = lax.broadcasted_iota(jnp.int32, (count, columns), 0)
    out = jnp.zeros((count, columns), F32)
    for row, term in enumerate(terms):
        out = jnp.where(at == row, term.astype(F32), out)
    return out.astype(BF16)


def stack_points(pts):
    scale = math.log2(math.e) / pts.shape[0]
    h, m, l = split3(pts)
    norm = jnp.sum(pts * pts, axis=0, keepdims=True) * (-scale)
    one = jnp.ones_like(norm)
    return jnp.concatenate([h, h, m, h, m, l, rows_of(16, [*split3(norm), one, one, one])], axis=0)


def stack_centres(cen):
    scale = math.log2(math.e) / cen.shape[0]
    h, m, l = split3(cen * (2.0 * scale))
    norm = jnp.sum(cen * cen, axis=0, keepdims=True) * (-scale)
    one = jnp.ones_like(norm)
    return jnp.concatenate([h, m, h, l, m, h, rows_of(16, [one, one, one, *split3(norm)])], axis=0)


def kernel(n, nblk, pts, cen, vdir, cnt, out, cbuf, pbuf, kbuf, inn, tbuf, rbuf, gs, gr, fs, ts, tr):
    width, slots = pts.shape
    cen_dev = cen.shape[1]
    blk = slots // nblk
    nch = n // 2
    me = lax.axis_index("dp")
    chip, core = lax.div(me, 2), lax.rem(me, 2)
    sibling = chip * 2 + 1 - core
    paired = nch & (nch - 1) == 0

    def flip(value, s):
        total, bit = 0, 1
        while bit < n:
            a, b = lax.rem(lax.div(value, bit), 2), (s // bit) % 2
            total = total + bit * (a + b - 2 * a * b)
            bit *= 2
        return total

    def chip_to(s):
        return flip(chip, s) if paired else lax.rem(chip + s, nch)

    def chip_from(s):
        return flip(chip, s) if paired else lax.rem(chip + nch - s, nch)

    barrier = pltpu.get_barrier_semaphore()
    for s in range(1, n):
        pl.semaphore_signal(barrier, inc=1, device_id={"dp": lax.rem(me + s, n)}, device_id_type=MESH)

    cbuf[me, :width, :] = cen[...]
    cbuf[me, width:, :] = jnp.concatenate([vdir[...], jnp.zeros((7, cen_dev), F32)], axis=0)
    pbuf[...] = stack_points(pts[...])
    pl.semaphore_wait(barrier, n - 1)

    def send_own(s):
        target = chip_to(s) * 2 + core if not (isinstance(s, int) and s == 0) else sibling
        return pltpu.make_async_remote_copy(
            src_ref=cbuf.at[me], dst_ref=cbuf.at[me], send_sem=gs.at[s], recv_sem=gr.at[me],
            device_id={"dp": target}, device_id_type=MESH)

    def forward(s):
        q = chip_from(s) * 2 + core
        return pltpu.make_async_remote_copy(
            src_ref=cbuf.at[q], dst_ref=cbuf.at[q], send_sem=fs.at[s], recv_sem=gr.at[q],
            device_id={"dp": sibling}, device_id_type=MESH)

    def wait_slot(q):
        pltpu.make_async_remote_copy(
            src_ref=cbuf.at[q], dst_ref=cbuf.at[q], send_sem=gs.at[0], recv_sem=gr.at[q],
            device_id={"dp": sibling}, device_id_type=MESH).wait_recv()

    def loop(start, stop, body):
        if stop - start <= 16:
            for s in range(start, stop):
                body(s)
        else:
            pl.loop(start, stop)(body)

    send_own(0).start()
    loop(1, nch, lambda s: send_own(s).start())

    def one_block(q, columns):
        held = cbuf[q]
        terms = stack_centres(held[:width])
        kern = jnp.exp2(lax.dot_general(
            terms, pbuf[:, columns], (((0,), (0,)), ((), ())), preferred_element_type=F32)).astype(BF16)
        kbuf[q] = kern
        weights = rows_of(16, split3(held[width:width + 1]))
        inn[...] += jnp.dot(weights, kern, preferred_element_type=F32)

    live = cnt[0]
    for part in range(nblk):
        columns = pl.ds(part * blk, blk)
        inn[...] = jnp.zeros_like(inn)
        one_block(me, columns)

        def step(s, part=part, columns=columns):
            near = chip_from(s) * 2 + core
            if part == 0:
                wait_slot(near)
                forward(s).start()
            one_block(near, columns)
            far = chip_from(s - 1) * 2 + 1 - core
            if part == 0:
                wait_slot(far)
            one_block(far, columns)

        loop(1, nch, step)
        last = chip_from(nch - 1) * 2 + 1 - core
        if part == 0:
            wait_slot(last)
        one_block(last, columns)

        sums = jnp.sum(inn[...], axis=0, keepdims=True) * (1.0 / math.sqrt(n * cen_dev))
        at = part * blk + lax.broadcasted_iota(jnp.int32, sums.shape, 1)
        inner = rows_of(16, [jnp.where(at < live, sums, 0.0)])

        def owner(s, part=part, inner=inner):
            q = lax.rem(me + s, n)
            term = lax.dot_general(
                inner, kbuf[q], (((1,), (1,)), ((), ())), preferred_element_type=F32)[:1]
            tbuf[q] = term if part == 0 else tbuf[q] + term
            if part == nblk - 1:
                send_term(s).start()

        def send_term(s):
            q = lax.rem(me + s, n)
            return pltpu.make_async_remote_copy(
                src_ref=tbuf.at[q], dst_ref=rbuf.at[me], send_sem=ts.at[s], recv_sem=tr.at[me],
                device_id={"dp": q}, device_id_type=MESH)

        loop(1, n, owner)
        mine = lax.dot_general(
            inner, kbuf[me], (((1,), (1,)), ((), ())), preferred_element_type=F32)[:1]
        tbuf[me] = mine if part == 0 else tbuf[me] + mine

    loop(0, nch, lambda s: send_own(s).wait_send())
    loop(1, nch, lambda s: forward(s).wait_send())
    out[...] = tbuf[me]

    def gather(s):
        q = lax.rem(me + s, n)
        pltpu.make_async_remote_copy(
            src_ref=tbuf.at[q], dst_ref=rbuf.at[q], send_sem=ts.at[s], recv_sem=tr.at[q],
            device_id={"dp": q}, device_id_type=MESH).wait()
        out[...] += rbuf[q]

    loop(1, n, gather)
    out[...] = out[...] * (1.0 / math.sqrt(slots * n))


def body(n, points, centres, direction, counts):
    width, slots = points.shape
    cen_dev = centres.shape[1]
    nblk = 1
    while n * cen_dev * (slots // nblk) * 2 > KERN_BYTES:
        nblk *= 2
    blk = slots // nblk
    depth = 6 * width + 16
    vmem = pl.BlockSpec(memory_space=pltpu.VMEM)
    got = pl.pallas_call(
        functools.partial(kernel, n, nblk),
        out_shape=jax.ShapeDtypeStruct((1, cen_dev), F32),
        in_specs=[vmem, vmem, vmem, pl.BlockSpec(memory_space=pltpu.SMEM)],
        out_specs=vmem,
        scratch_shapes=[
            pltpu.VMEM((n, width + 8, cen_dev), F32),
            pltpu.VMEM((depth, slots), BF16),
            pltpu.VMEM((n, cen_dev, blk), BF16),
            pltpu.VMEM((16, blk), F32),
            pltpu.VMEM((n, 1, cen_dev), F32),
            pltpu.VMEM((n, 1, cen_dev), F32),
            pltpu.SemaphoreType.DMA((n,)),
            pltpu.SemaphoreType.DMA((n,)),
            pltpu.SemaphoreType.DMA((n,)),
            pltpu.SemaphoreType.DMA((n,)),
            pltpu.SemaphoreType.DMA((n,)),
        ],
        compiler_params=pltpu.CompilerParams(
            collective_id=0, has_side_effects=True, vmem_limit_bytes=48 << 20),
        cost_estimate=pl.CostEstimate(
            flops=2 * slots * n * cen_dev * (depth + 2), bytes_accessed=4 * width * (slots + cen_dev),
            transcendentals=slots * n * cen_dev),
    )(points, centres, direction.reshape(1, cen_dev), counts)
    return got.reshape(cen_dev)


def solution(mesh):
    placed = (
        P(None, ("groups", "dp")),
        P(None, ("groups", "dp")),
        P(("groups", "dp")),
        P(("groups", "dp")),
    )
    return jax.shard_map(
        functools.partial(body, mesh.shape["dp"]), mesh=mesh, in_specs=placed,
        out_specs=P(("groups", "dp")), check_vma=False)
```

```python
import functools
import math

import jax
import jax.numpy as jnp
from jax import lax
from jax.experimental import pallas as pl
from jax.experimental.pallas import tpu as pltpu
from jax.sharding import PartitionSpec as P

MESH = pl.DeviceIdType.MESH
KERN_BYTES = 16 << 20
F32, BF16 = jnp.float32, jnp.bfloat16


def split3(x):
    high = x.astype(BF16)
    rest = x - high.astype(F32)
    mid = rest.astype(BF16)
    low = (rest - mid.astype(F32)).astype(BF16)
    return high, mid, low


def rows_of(count, terms):
    columns = terms[0].shape[1]
    at = lax.broadcasted_iota(jnp.int32, (count, columns), 0)
    out = jnp.zeros((count, columns), F32)
    for row, term in enumerate(terms):
        out = jnp.where(at == row, term.astype(F32), out)
    return out.astype(BF16)


def stack_points(pts):
    scale = math.log2(math.e) / pts.shape[0]
    h, m, l = split3(pts)
    norm = jnp.sum(pts * pts, axis=0, keepdims=True) * (-scale)
    one = jnp.ones_like(norm)
    return jnp.concatenate([h, h, m, h, m, l, rows_of(16, [*split3(norm), one, one, one])], axis=0)


def stack_centres(cen):
    scale = math.log2(math.e) / cen.shape[0]
    h, m, l = split3(cen * (2.0 * scale))
    norm = jnp.sum(cen * cen, axis=0, keepdims=True) * (-scale)
    one = jnp.ones_like(norm)
    return jnp.concatenate([h, m, h, l, m, h, rows_of(16, [one, one, one, *split3(norm)])], axis=0)


def kernel(nch, nblk, pts, cen, vdir, cnt, out, pshare, cbuf, drow, live, pbuf, kbuf, inn, ibuf, tbuf, rbuf,
           ls, ps, gs, gr, es, er, ts, tr):
    width, slots = pts.shape
    cen_dev = cen.shape[1]
    blk = slots // nblk
    me = lax.axis_index("dp")
    chip, core = lax.div(me, 2), lax.rem(me, 2)
    other = 1 - core
    sibling = {"dp": chip * 2 + other}
    paired = nch & (nch - 1) == 0

    def flip(value, s):
        total, bit = 0, 1
        while bit < nch:
            a, b = lax.rem(lax.div(value, bit), 2), (s // bit) % 2
            total = total + bit * (a + b - 2 * a * b)
            bit *= 2
        return total

    def chip_to(s):
        return flip(chip, s) if paired else lax.rem(chip + s, nch)

    def chip_from(s):
        return flip(chip, s) if paired else lax.rem(chip + nch - s, nch)

    def peer(c):
        return {"dp": c * 2 + core}

    def loop(start, stop, body):
        if stop - start <= 16:
            for s in range(start, stop):
                body(s)
        else:
            pl.loop(start, stop)(body)

    def copy(src, dst, send, recv, device):
        return pltpu.make_async_remote_copy(
            src_ref=src, dst_ref=dst, send_sem=send, recv_sem=recv, device_id=device, device_id_type=MESH)

    barrier = pltpu.get_barrier_semaphore()
    loop(1, nch, lambda s: pl.semaphore_signal(
        barrier, inc=1, device_id=peer(chip_to(nch - s)), device_id_type=MESH))
    pl.semaphore_signal(barrier, inc=1, device_id=sibling, device_id_type=MESH)

    loads = [
        pltpu.make_async_copy(cen, cbuf.at[chip, :width], ls.at[0]),
        pltpu.make_async_copy(vdir, drow, ls.at[1]),
        pltpu.make_async_copy(cnt, live, ls.at[2]),
        pltpu.make_async_copy(pts, pshare.at[core, :width], ls.at[3]),
    ]
    for load in loads:
        load.start()
    for load in loads:
        load.wait()
    cbuf[chip, width:, :] = jnp.broadcast_to(drow[...], (8, cen_dev))
    at = lax.broadcasted_iota(jnp.int32, (8, slots), 1)
    pshare[core, width:, :] = jnp.where(at < live[0], 1.0, 0.0).astype(F32)

    def send_own(s):
        return copy(cbuf.at[chip], cbuf.at[chip], gs.at[s], gr.at[chip], peer(chip_to(s)))

    share = copy(pshare.at[core], pshare.at[core], ps.at[0], ps.at[1], sibling)

    def wait_slot(q):
        copy(cbuf.at[q], cbuf.at[q], gs.at[0], gr.at[q], sibling).wait_recv()

    def exchange(part):
        return copy(ibuf.at[part, 0], ibuf.at[part, 1], es.at[part], er.at[part], sibling)

    def send_term(s):
        q = chip_to(s)
        return copy(tbuf.at[q], rbuf.at[chip], ts.at[s], tr.at[chip], peer(q))

    def one_block(q, terms, weights, half, part):
        kern = jnp.exp2(lax.dot_general(
            terms, pbuf[half, :, pl.ds(part * blk, blk)], (((0,), (0,)), ((), ())),
            preferred_element_type=F32)).astype(BF16)
        kbuf[q, half] = kern
        inn[half] += jnp.dot(weights, kern, preferred_element_type=F32)

    def stacked(q):
        held = cbuf[q]
        return stack_centres(held[:width]), rows_of(16, split3(held[width:width + 1]))

    for part in range(nblk):
        inn[...] = jnp.zeros_like(inn)
        if part == 0:
            pl.semaphore_wait(barrier, nch)
            share.start()
            loop(1, nch, lambda s: send_own(nch - s).start())
            pbuf[core] = stack_points(pshare[core, :width, :])
        one_block(chip, *stacked(chip), core, part)
        if part == 0:
            share.wait_recv()
            pbuf[other] = stack_points(pshare[other, :width, :])
        one_block(chip, *stacked(chip), other, part)

        def step(s, part=part):
            q = chip_from(s)
            if part == 0:
                wait_slot(q)
            terms, weights = stacked(q)
            one_block(q, terms, weights, 0, part)
            one_block(q, terms, weights, 1, part)

        loop(1, nch, step)

        ibuf[part, 0] = jnp.sum(inn[...], axis=1, keepdims=True)
        exchange(part).start()
        exchange(part).wait_recv()
        inner = []
        for half in range(2):
            sums = (ibuf[part, 0, half] + ibuf[part, 1, half]) * (1.0 / math.sqrt(nch * 2 * cen_dev))
            mask = pshare[half, width:width + 1, pl.ds(part * blk, blk)]
            inner.append(rows_of(16, [jnp.where(mask > 0.5, sums, 0.0)]))

        def product(q, part=part, inner=inner):
            term = 0.0
            for half in range(2):
                term = term + lax.dot_general(
                    inner[half], kbuf[q, half], (((1,), (1,)), ((), ())), preferred_element_type=F32)[:1]
            tbuf[q] = term if part == 0 else tbuf[q] + term

        def owner(s, part=part):
            product(chip_to(nch - s))
            if part == nblk - 1:
                send_term(nch - s).start()

        loop(1, nch, owner)
        product(chip)

    share.wait_send()
    loop(1, nch, lambda s: send_own(s).wait_send())
    for part in range(nblk):
        exchange(part).wait_send()
    out[...] = tbuf[chip]

    def gather(s):
        q = chip_from(s)
        copy(tbuf.at[q], rbuf.at[q], ts.at[s], tr.at[q], peer(q)).wait()
        out[...] += rbuf[q]

    loop(1, nch, gather)
    out[...] = out[...] * (1.0 / math.sqrt(slots * nch * 2))


def body(n, points, centres, direction, counts):
    width, slots = points.shape
    cen_dev = centres.shape[1]
    nch = n // 2
    nblk = 1
    while nch * cen_dev * 2 * (slots // nblk) * 2 > KERN_BYTES:
        nblk *= 2
    blk = slots // nblk
    depth = 6 * width + 16
    hbm = pl.BlockSpec(memory_space=pl.ANY)
    sem = pltpu.SemaphoreType.DMA
    got = pl.pallas_call(
        functools.partial(kernel, nch, nblk),
        out_shape=jax.ShapeDtypeStruct((1, cen_dev), F32),
        in_specs=[hbm, hbm, hbm, hbm],
        out_specs=pl.BlockSpec(memory_space=pltpu.VMEM),
        scratch_shapes=[
            pltpu.VMEM((2, width + 8, slots), F32),
            pltpu.VMEM((nch, width + 8, cen_dev), F32),
            pltpu.VMEM((1, cen_dev), F32),
            pltpu.SMEM((1,), jnp.int32),
            pltpu.VMEM((2, depth, slots), BF16),
            pltpu.VMEM((nch, 2, cen_dev, blk), BF16),
            pltpu.VMEM((2, 16, blk), F32),
            pltpu.VMEM((nblk, 2, 2, 1, blk), F32),
            pltpu.VMEM((nch, 1, cen_dev), F32),
            pltpu.VMEM((nch, 1, cen_dev), F32),
            sem((4,)), sem((2,)), sem((nch,)), sem((nch,)), sem((nblk,)), sem((nblk,)), sem((nch,)), sem((nch,)),
        ],
        compiler_params=pltpu.CompilerParams(
            collective_id=0, has_side_effects=True, vmem_limit_bytes=48 << 20),
        cost_estimate=pl.CostEstimate(
            flops=2 * slots * n * cen_dev * (depth + 2), bytes_accessed=4 * width * (slots + cen_dev),
            transcendentals=slots * n * cen_dev),
    )(points, centres, direction.reshape(1, cen_dev), counts)
    return got.reshape(cen_dev)


def solution(mesh):
    placed = (
        P(None, ("groups", "dp")),
        P(None, ("groups", "dp")),
        P(("groups", "dp")),
        P(("groups", "dp")),
    )
    return jax.shard_map(
        functools.partial(body, mesh.shape["dp"]), mesh=mesh, in_specs=placed,
        out_specs=P(("groups", "dp")), check_vma=False)
```

```python
import functools
import math

import jax
import jax.numpy as jnp
from jax import lax
from jax.experimental import pallas as pl
from jax.experimental.pallas import tpu as pltpu
from jax.sharding import PartitionSpec as P

MESH = pl.DeviceIdType.MESH
KERN_BYTES = 16 << 20
F32, BF16 = jnp.float32, jnp.bfloat16


def split3(x):
    high = x.astype(BF16)
    rest = x - high.astype(F32)
    mid = rest.astype(BF16)
    low = (rest - mid.astype(F32)).astype(BF16)
    return high, mid, low


def rows_of(count, terms):
    columns = terms[0].shape[1]
    at = lax.broadcasted_iota(jnp.int32, (count, columns), 0)
    out = jnp.zeros((count, columns), F32)
    for row, term in enumerate(terms):
        out = jnp.where(at == row, term.astype(F32), out)
    return out.astype(BF16)


def stack_points(pts):
    scale = math.log2(math.e) / pts.shape[0]
    h, m, l = split3(pts)
    norm = jnp.sum(pts * pts, axis=0, keepdims=True) * (-scale)
    one = jnp.ones_like(norm)
    return jnp.concatenate([h, h, m, h, m, l, rows_of(16, [*split3(norm), one, one, one])], axis=0)


def stack_centres(cen):
    scale = math.log2(math.e) / cen.shape[0]
    h, m, l = split3(cen * (2.0 * scale))
    norm = jnp.sum(cen * cen, axis=0, keepdims=True) * (-scale)
    one = jnp.ones_like(norm)
    return jnp.concatenate([h, m, h, l, m, h, rows_of(16, [one, one, one, *split3(norm)])], axis=0)


def kernel(nch, nblk, pts, cen, vdir, cnt, out, pshare, cbuf, dbuf, live, pbuf, kbuf, inn, ibuf, tbuf, rbuf,
           ls, ps, gs, gr, fs, ds, dr, es, er, ts, tr):
    width, slots = pts.shape
    cen_dev = cen.shape[1]
    blk = slots // nblk
    me = lax.axis_index("dp")
    chip, core = lax.div(me, 2), lax.rem(me, 2)
    other = 1 - core
    sibling = {"dp": chip * 2 + other}
    paired = nch & (nch - 1) == 0

    def flip(value, s):
        total, bit = 0, 1
        while bit < nch:
            a, b = lax.rem(lax.div(value, bit), 2), (s // bit) % 2
            total = total + bit * (a + b - 2 * a * b)
            bit *= 2
        return total

    def chip_to(s):
        return flip(chip, s) if paired else lax.rem(chip + s, nch)

    def chip_from(s):
        return flip(chip, s) if paired else lax.rem(chip + nch - s, nch)

    def peer(c):
        return {"dp": c * 2 + core}

    def loop(start, stop, body):
        if stop - start <= 16:
            for s in range(start, stop):
                body(s)
        else:
            pl.loop(start, stop)(body)

    def copy(src, dst, send, recv, device):
        return pltpu.make_async_remote_copy(
            src_ref=src, dst_ref=dst, send_sem=send, recv_sem=recv, device_id=device, device_id_type=MESH)

    barrier = pltpu.get_barrier_semaphore()
    loop(1, nch, lambda s: pl.semaphore_signal(
        barrier, inc=1, device_id=peer(chip_to(nch - s)), device_id_type=MESH))
    pl.semaphore_signal(barrier, inc=1, device_id=sibling, device_id_type=MESH)

    loads = [
        pltpu.make_async_copy(cen, cbuf.at[chip], ls.at[0]),
        pltpu.make_async_copy(vdir, dbuf.at[chip], ls.at[1]),
        pltpu.make_async_copy(cnt, live, ls.at[2]),
        pltpu.make_async_copy(pts, pshare.at[core, :width], ls.at[3]),
    ]
    for load in loads:
        load.start()
    for load in loads:
        load.wait()
    at = lax.broadcasted_iota(jnp.int32, (8, slots), 1)
    pshare[core, width:, :] = jnp.where(at < live[0], 1.0, 0.0).astype(F32)

    def send_own(s):
        return copy(cbuf.at[chip], cbuf.at[chip], gs.at[s], gr.at[chip], peer(chip_to(s)))

    def send_direction(s):
        return copy(dbuf.at[chip], dbuf.at[chip], ds.at[s], dr.at[chip], peer(chip_to(s)))

    def forward(s):
        q = chip_from(s)
        return copy(cbuf.at[q], cbuf.at[q], fs.at[s], gr.at[q], peer(chip_to(1)))

    share = copy(pshare.at[core], pshare.at[core], ps.at[0], ps.at[1], sibling)

    def wait_slot(q):
        copy(cbuf.at[q], cbuf.at[q], gs.at[0], gr.at[q], sibling).wait_recv()

    def wait_direction(q):
        copy(dbuf.at[q], dbuf.at[q], ds.at[0], dr.at[q], sibling).wait_recv()

    def exchange(part):
        return copy(ibuf.at[part, 0], ibuf.at[part, 1], es.at[part], er.at[part], sibling)

    def send_term(s):
        q = chip_to(s)
        return copy(tbuf.at[q], rbuf.at[chip], ts.at[s], tr.at[chip], peer(q))

    def one_block(q, terms, weights, half, part):
        kern = jnp.exp2(lax.dot_general(
            terms, pbuf[half, :, pl.ds(part * blk, blk)], (((0,), (0,)), ((), ())),
            preferred_element_type=F32)).astype(BF16)
        kbuf[q, half] = kern
        inn[half] += jnp.dot(weights, kern, preferred_element_type=F32)

    def stacked(q):
        return stack_centres(cbuf[q]), rows_of(16, split3(dbuf[q]))

    direct = [s for s in range(nch) if s == 1 or s % 2 == 0][1:]
    for part in range(nblk):
        inn[...] = jnp.zeros_like(inn)
        if part == 0:
            pbuf[core] = stack_points(pshare[core, :width, :])
            pl.semaphore_wait(barrier, nch)
            for s in direct[1:]:
                send_own(s).start()
            send_own(1).start()
            share.start()
            loop(1, nch, lambda s: send_direction(nch - s).start())
        one_block(chip, *stacked(chip), core, part)
        if part == 0:
            share.wait_recv()
            pbuf[other] = stack_points(pshare[other, :width, :])
        one_block(chip, *stacked(chip), other, part)

        def both(q, part=part):
            if part == 0:
                wait_direction(q)
            terms, weights = stacked(q)
            one_block(q, terms, weights, 0, part)
            one_block(q, terms, weights, 1, part)

        def step(k, part=part):
            near, far = chip_from(2 * k), chip_from(2 * k - 1)
            if part == 0:
                wait_slot(near)
                forward(2 * k).start()
                wait_slot(far)
            both(far)
            both(near)

        loop(1, nch // 2, step)
        if part == 0:
            wait_slot(chip_from(nch - 1))
        both(chip_from(nch - 1))

        ibuf[part, 0] = jnp.sum(inn[...], axis=1, keepdims=True)
        exchange(part).start()
        exchange(part).wait_recv()
        inner = []
        for half in range(2):
            sums = (ibuf[part, 0, half] + ibuf[part, 1, half]) * (1.0 / math.sqrt(nch * 2 * cen_dev))
            mask = pshare[half, width:width + 1, pl.ds(part * blk, blk)]
            inner.append(rows_of(16, [jnp.where(mask > 0.5, sums, 0.0)]))

        def product(q, part=part, inner=inner):
            term = 0.0
            for half in range(2):
                term = term + lax.dot_general(
                    inner[half], kbuf[q, half], (((1,), (1,)), ((), ())), preferred_element_type=F32)[:1]
            tbuf[q] = term if part == 0 else tbuf[q] + term

        def owner(s, part=part):
            product(chip_to(nch - s))
            if part == nblk - 1:
                send_term(nch - s).start()

        loop(1, nch, owner)
        product(chip)

    share.wait_send()
    for s in direct:
        send_own(s).wait_send()
    loop(1, nch // 2, lambda k: forward(2 * k).wait_send())
    loop(1, nch, lambda s: send_direction(s).wait_send())
    for part in range(nblk):
        exchange(part).wait_send()
    out[...] = tbuf[chip]

    def gather(s):
        q = chip_from(s)
        copy(tbuf.at[q], rbuf.at[q], ts.at[s], tr.at[q], peer(q)).wait()
        out[...] += rbuf[q]

    loop(1, nch, gather)
    out[...] = out[...] * (1.0 / math.sqrt(slots * nch * 2))


def body(n, points, centres, direction, counts):
    width, slots = points.shape
    cen_dev = centres.shape[1]
    nch = n // 2
    nblk = 1
    while nch * cen_dev * 2 * (slots // nblk) * 2 > KERN_BYTES:
        nblk *= 2
    blk = slots // nblk
    depth = 6 * width + 16
    hbm = pl.BlockSpec(memory_space=pltpu.HBM)
    sem = pltpu.SemaphoreType.DMA
    got = pl.pallas_call(
        functools.partial(kernel, nch, nblk),
        out_shape=jax.ShapeDtypeStruct((1, cen_dev), F32),
        in_specs=[hbm, hbm, hbm, hbm],
        out_specs=pl.BlockSpec(memory_space=pltpu.VMEM),
        scratch_shapes=[
            pltpu.VMEM((2, width + 8, slots), F32),
            pltpu.VMEM((nch, width, cen_dev), F32),
            pltpu.VMEM((nch, 1, cen_dev), F32),
            pltpu.SMEM((1,), jnp.int32),
            pltpu.VMEM((2, depth, slots), BF16),
            pltpu.VMEM((nch, 2, cen_dev, blk), BF16),
            pltpu.VMEM((2, 16, blk), F32),
            pltpu.VMEM((nblk, 2, 2, 1, blk), F32),
            pltpu.VMEM((nch, 1, cen_dev), F32),
            pltpu.VMEM((nch, 1, cen_dev), F32),
            sem((4,)), sem((2,)), sem((nch,)), sem((nch,)), sem((nch,)), sem((nch,)), sem((nch,)), sem((nblk,)), sem((nblk,)), sem((nch,)), sem((nch,)),
        ],
        compiler_params=pltpu.CompilerParams(
            collective_id=0, has_side_effects=True, vmem_limit_bytes=48 << 20),
        cost_estimate=pl.CostEstimate(
            flops=2 * slots * n * cen_dev * (depth + 2), bytes_accessed=4 * width * (slots + cen_dev),
            transcendentals=slots * n * cen_dev),
    )(points, centres, direction.reshape(1, cen_dev), counts)
    return got.reshape(cen_dev)


def solution(mesh):
    placed = (
        P(None, ("groups", "dp")),
        P(None, ("groups", "dp")),
        P(("groups", "dp")),
        P(("groups", "dp")),
    )
    return jax.shard_map(
        functools.partial(body, mesh.shape["dp"]), mesh=mesh, in_specs=placed,
        out_specs=P(("groups", "dp")), check_vma=False)
```

```python
import functools
import math

import jax
import jax.numpy as jnp
from jax import lax
from jax.experimental import pallas as pl
from jax.experimental.pallas import tpu as pltpu
from jax.sharding import PartitionSpec as P

MESH = pl.DeviceIdType.MESH
KERN_BYTES = 16 << 20
F32, BF16 = jnp.float32, jnp.bfloat16


def split3(x):
    high = x.astype(BF16)
    rest = x - high.astype(F32)
    mid = rest.astype(BF16)
    low = (rest - mid.astype(F32)).astype(BF16)
    return high, mid, low


def rows_of(count, terms):
    columns = terms[0].shape[1]
    at = lax.broadcasted_iota(jnp.int32, (count, columns), 0)
    out = jnp.zeros((count, columns), F32)
    for row, term in enumerate(terms):
        out = jnp.where(at == row, term.astype(F32), out)
    return out.astype(BF16)


def stack_points(pts):
    scale = math.log2(math.e) / pts.shape[0]
    h, m, l = split3(pts)
    norm = jnp.sum(pts * pts, axis=0, keepdims=True) * (-scale)
    one = jnp.ones_like(norm)
    return jnp.concatenate([h, h, m, h, m, l, rows_of(16, [*split3(norm), one, one, one])], axis=0)


def stack_centres(cen):
    scale = math.log2(math.e) / cen.shape[0]
    h, m, l = split3(cen * (2.0 * scale))
    norm = jnp.sum(cen * cen, axis=0, keepdims=True) * (-scale)
    one = jnp.ones_like(norm)
    return jnp.concatenate([h, m, h, l, m, h, rows_of(16, [one, one, one, *split3(norm)])], axis=0)


def kernel(nch, nblk, pts, cen, vdir, cnt, out, pshare, cbuf, dbuf, live, pbuf, kbuf, inn, ibuf, tbuf, rbuf,
           ls, ps, gs, gr, ds, dr, es, er, ts, tr):
    width, slots = pts.shape
    cen_dev = cen.shape[1]
    blk = slots // nblk
    me = lax.axis_index("dp")
    chip, core = lax.div(me, 2), lax.rem(me, 2)
    other = 1 - core
    sibling = {"dp": chip * 2 + other}
    paired = nch & (nch - 1) == 0

    def flip(value, s):
        total, bit = 0, 1
        while bit < nch:
            a, b = lax.rem(lax.div(value, bit), 2), (s // bit) % 2
            total = total + bit * (a + b - 2 * a * b)
            bit *= 2
        return total

    def chip_to(s):
        return flip(chip, s) if paired else lax.rem(chip + s, nch)

    def chip_from(s):
        return flip(chip, s) if paired else lax.rem(chip + nch - s, nch)

    def peer(c):
        return {"dp": c * 2 + core}

    def loop(start, stop, body):
        if stop - start <= 16:
            for s in range(start, stop):
                body(s)
        else:
            pl.loop(start, stop)(body)

    def copy(src, dst, send, recv, device):
        return pltpu.make_async_remote_copy(
            src_ref=src, dst_ref=dst, send_sem=send, recv_sem=recv, device_id=device, device_id_type=MESH)

    barrier = pltpu.get_barrier_semaphore()
    loop(1, nch, lambda s: pl.semaphore_signal(
        barrier, inc=1, device_id=peer(chip_to(nch - s)), device_id_type=MESH))
    pl.semaphore_signal(barrier, inc=1, device_id=sibling, device_id_type=MESH)

    loads = [
        pltpu.make_async_copy(cen, cbuf.at[chip], ls.at[0]),
        pltpu.make_async_copy(vdir, dbuf.at[chip], ls.at[1]),
        pltpu.make_async_copy(cnt, live, ls.at[2]),
        pltpu.make_async_copy(pts, pshare.at[core, :width], ls.at[3]),
    ]
    for load in loads:
        load.start()
    for load in loads:
        load.wait()
    at = lax.broadcasted_iota(jnp.int32, (8, slots), 1)
    pshare[core, width:, :] = jnp.where(at < live[0], 1.0, 0.0).astype(F32)

    def send_own(s):
        return copy(cbuf.at[chip], cbuf.at[chip], gs.at[s], gr.at[chip], peer(chip_to(s)))

    def send_direction(s):
        return copy(dbuf.at[chip], dbuf.at[chip], ds.at[s], dr.at[chip], peer(chip_to(s)))

    share = copy(pshare.at[core], pshare.at[core], ps.at[0], ps.at[1], sibling)

    def wait_slot(q):
        copy(cbuf.at[q], cbuf.at[q], gs.at[0], gr.at[q], sibling).wait_recv()

    def wait_direction(q):
        copy(dbuf.at[q], dbuf.at[q], ds.at[0], dr.at[q], sibling).wait_recv()

    def exchange(part):
        return copy(ibuf.at[part, 0], ibuf.at[part, 1], es.at[part], er.at[part], sibling)

    def send_term(s):
        q = chip_to(s)
        return copy(tbuf.at[q], rbuf.at[chip], ts.at[s], tr.at[chip], peer(q))

    def one_block(q, terms, weights, half, part):
        kern = jnp.exp2(lax.dot_general(
            terms, pbuf[half, :, pl.ds(part * blk, blk)], (((0,), (0,)), ((), ())),
            preferred_element_type=F32)).astype(BF16)
        kbuf[q, half] = kern
        inn[half] += jnp.dot(weights, kern, preferred_element_type=F32)

    def stacked(q):
        return stack_centres(cbuf[q]), rows_of(16, split3(dbuf[q]))

    for part in range(nblk):
        inn[...] = jnp.zeros_like(inn)
        if part == 0:
            pbuf[core] = stack_points(pshare[core, :width, :])
            pl.semaphore_wait(barrier, nch)
            share.start()
            loop(1, nch, lambda s: send_own(s).start())
            loop(1, nch, lambda s: send_direction(nch - s).start())
        one_block(chip, *stacked(chip), core, part)
        if part == 0:
            share.wait_recv()
            pbuf[other] = stack_points(pshare[other, :width, :])
        one_block(chip, *stacked(chip), other, part)

        def both(q, part=part):
            if part == 0:
                wait_direction(q)
            terms, weights = stacked(q)
            one_block(q, terms, weights, 0, part)
            one_block(q, terms, weights, 1, part)

        def step(s, part=part):
            q = chip_from(s)
            if part == 0:
                wait_slot(q)
            both(q)

        loop(1, nch, step)

        ibuf[part, 0] = jnp.sum(inn[...], axis=1, keepdims=True)
        exchange(part).start()
        exchange(part).wait_recv()
        inner = []
        for half in range(2):
            sums = (ibuf[part, 0, half] + ibuf[part, 1, half]) * (1.0 / math.sqrt(nch * 2 * cen_dev))
            mask = pshare[half, width:width + 1, pl.ds(part * blk, blk)]
            inner.append(rows_of(16, [jnp.where(mask > 0.5, sums, 0.0)]))

        def product(q, part=part, inner=inner):
            term = 0.0
            for half in range(2):
                term = term + lax.dot_general(
                    inner[half], kbuf[q, half], (((1,), (1,)), ((), ())), preferred_element_type=F32)[:1]
            tbuf[q] = term if part == 0 else tbuf[q] + term

        def owner(s, part=part):
            product(chip_to(nch - s))
            if part == nblk - 1:
                send_term(nch - s).start()

        loop(1, nch, owner)
        product(chip)

    share.wait_send()
    loop(1, nch, lambda s: send_own(s).wait_send())
    loop(1, nch, lambda s: send_direction(s).wait_send())
    for part in range(nblk):
        exchange(part).wait_send()
    out[...] = tbuf[chip]

    def gather(s):
        q = chip_from(s)
        copy(tbuf.at[q], rbuf.at[q], ts.at[s], tr.at[q], peer(q)).wait()
        out[...] += rbuf[q]

    loop(1, nch, gather)
    out[...] = out[...] * (1.0 / math.sqrt(slots * nch * 2))


def body(n, points, centres, direction, counts):
    width, slots = points.shape
    cen_dev = centres.shape[1]
    nch = n // 2
    nblk = 1
    while nch * cen_dev * 2 * (slots // nblk) * 2 > KERN_BYTES:
        nblk *= 2
    blk = slots // nblk
    depth = 6 * width + 16
    hbm = pl.BlockSpec(memory_space=pltpu.HBM)
    sem = pltpu.SemaphoreType.DMA
    got = pl.pallas_call(
        functools.partial(kernel, nch, nblk),
        out_shape=jax.ShapeDtypeStruct((1, cen_dev), F32),
        in_specs=[hbm, hbm, hbm, hbm],
        out_specs=pl.BlockSpec(memory_space=pltpu.VMEM),
        scratch_shapes=[
            pltpu.VMEM((2, width + 8, slots), F32),
            pltpu.VMEM((nch, width, cen_dev), F32),
            pltpu.VMEM((nch, 1, cen_dev), F32),
            pltpu.SMEM((1,), jnp.int32),
            pltpu.VMEM((2, depth, slots), BF16),
            pltpu.VMEM((nch, 2, cen_dev, blk), BF16),
            pltpu.VMEM((2, 16, blk), F32),
            pltpu.VMEM((nblk, 2, 2, 1, blk), F32),
            pltpu.VMEM((nch, 1, cen_dev), F32),
            pltpu.VMEM((nch, 1, cen_dev), F32),
            sem((4,)), sem((2,)), sem((nch,)), sem((nch,)), sem((nch,)), sem((nch,)), sem((nblk,)), sem((nblk,)), sem((nch,)), sem((nch,)),
        ],
        compiler_params=pltpu.CompilerParams(
            collective_id=0, has_side_effects=True, vmem_limit_bytes=63 << 20),
        cost_estimate=pl.CostEstimate(
            flops=2 * slots * n * cen_dev * (depth + 2), bytes_accessed=4 * width * (slots + cen_dev),
            transcendentals=slots * n * cen_dev),
    )(points, centres, direction.reshape(1, cen_dev), counts)
    return got.reshape(cen_dev)


def solution(mesh):
    placed = (
        P(None, ("groups", "dp")),
        P(None, ("groups", "dp")),
        P(("groups", "dp")),
        P(("groups", "dp")),
    )
    return jax.shard_map(
        functools.partial(body, mesh.shape["dp"]), mesh=mesh, in_specs=placed,
        out_specs=P(("groups", "dp")), check_vma=False)
```

```python
import functools
import math

import jax
import jax.numpy as jnp
from jax import lax
from jax.experimental import pallas as pl
from jax.experimental.pallas import tpu as pltpu
from jax.sharding import PartitionSpec as P

MESH = pl.DeviceIdType.MESH
KERN_BYTES = 16 << 20
F32, BF16 = jnp.float32, jnp.bfloat16


def split3(x):
    high = x.astype(BF16)
    rest = x - high.astype(F32)
    mid = rest.astype(BF16)
    low = (rest - mid.astype(F32)).astype(BF16)
    return high, mid, low


def rows_of(count, terms):
    columns = terms[0].shape[1]
    at = lax.broadcasted_iota(jnp.int32, (count, columns), 0)
    out = jnp.zeros((count, columns), F32)
    for row, term in enumerate(terms):
        out = jnp.where(at == row, term.astype(F32), out)
    return out.astype(BF16)


def stack_points(pts):
    scale = math.log2(math.e) / pts.shape[0]
    h, m, l = split3(pts)
    norm = jnp.sum(pts * pts, axis=0, keepdims=True) * (-scale)
    one = jnp.ones_like(norm)
    return jnp.concatenate([h, h, m, h, m, l, rows_of(16, [*split3(norm), one, one, one])], axis=0)


def stack_centres(cen):
    scale = math.log2(math.e) / cen.shape[0]
    h, m, l = split3(cen * (2.0 * scale))
    norm = jnp.sum(cen * cen, axis=0, keepdims=True) * (-scale)
    one = jnp.ones_like(norm)
    return jnp.concatenate([h, m, h, l, m, h, rows_of(16, [one, one, one, *split3(norm)])], axis=0)


def kernel(nch, nblk, pts, cen, vdir, cnt, out, pshare, cbuf, dbuf, live, pbuf, kbuf, inn, ibuf, tbuf, rbuf,
           ls, ps, gs, gr, ds, dr, es, er, ts, tr):
    width, slots = pts.shape
    cen_dev = cen.shape[1]
    blk = slots // nblk
    me = lax.axis_index("dp")
    chip, core = lax.div(me, 2), lax.rem(me, 2)
    other = 1 - core
    sibling = {"dp": chip * 2 + other}
    paired = nch & (nch - 1) == 0

    def flip(value, s):
        total, bit = 0, 1
        while bit < nch:
            a, b = lax.rem(lax.div(value, bit), 2), (s // bit) % 2
            total = total + bit * (a + b - 2 * a * b)
            bit *= 2
        return total

    def chip_to(s):
        return flip(chip, s) if paired else lax.rem(chip + s, nch)

    def chip_from(s):
        return flip(chip, s) if paired else lax.rem(chip + nch - s, nch)

    def peer(c):
        return {"dp": c * 2 + core}

    def loop(start, stop, body):
        if stop - start <= 16:
            for s in range(start, stop):
                body(s)
        else:
            pl.loop(start, stop)(body)

    def copy(src, dst, send, recv, device):
        return pltpu.make_async_remote_copy(
            src_ref=src, dst_ref=dst, send_sem=send, recv_sem=recv, device_id=device, device_id_type=MESH)

    barrier = pltpu.get_barrier_semaphore()
    loop(1, nch, lambda s: pl.semaphore_signal(
        barrier, inc=1, device_id=peer(chip_to(nch - s)), device_id_type=MESH))
    pl.semaphore_signal(barrier, inc=1, device_id=sibling, device_id_type=MESH)

    loads = [
        pltpu.make_async_copy(cen, cbuf.at[chip], ls.at[0]),
        pltpu.make_async_copy(vdir, dbuf.at[chip], ls.at[1]),
        pltpu.make_async_copy(cnt, live, ls.at[2]),
        pltpu.make_async_copy(pts, pshare.at[core, :width], ls.at[3]),
    ]
    for load in loads:
        load.start()
    for load in loads:
        load.wait()
    at = lax.broadcasted_iota(jnp.int32, (8, slots), 1)
    pshare[core, width:, :] = jnp.where(at < live[0], 1.0, 0.0).astype(F32)

    def send_own(s):
        return copy(cbuf.at[chip], cbuf.at[chip], gs.at[s], gr.at[chip], peer(chip_to(s)))

    def send_direction(s):
        return copy(dbuf.at[chip], dbuf.at[chip], ds.at[s], dr.at[chip], peer(chip_to(s)))

    share = copy(pshare.at[core], pshare.at[core], ps.at[0], ps.at[1], sibling)

    def wait_slot(q):
        copy(cbuf.at[q], cbuf.at[q], gs.at[0], gr.at[q], sibling).wait_recv()

    def wait_direction(q):
        copy(dbuf.at[q], dbuf.at[q], ds.at[0], dr.at[q], sibling).wait_recv()

    def exchange(part):
        return copy(ibuf.at[part, 0], ibuf.at[part, 1], es.at[part], er.at[part], sibling)

    def send_term(s):
        q = chip_to(s)
        return copy(tbuf.at[q], rbuf.at[chip], ts.at[s], tr.at[chip], peer(q))

    def one_block(q, terms, weights, half, part):
        kern = jnp.exp2(lax.dot_general(
            terms, pbuf[half, :, pl.ds(part * blk, blk)], (((0,), (0,)), ((), ())),
            preferred_element_type=F32)).astype(BF16)
        kbuf[q, half] = kern
        inn[half] += jnp.dot(weights, kern, preferred_element_type=F32)

    def stacked(q):
        return stack_centres(cbuf[q]), rows_of(16, split3(dbuf[q]))

    for part in range(nblk):
        inn[...] = jnp.zeros_like(inn)
        if part == 0:
            pbuf[core] = stack_points(pshare[core, :width, :])
            pl.semaphore_wait(barrier, nch)
            loop(1, nch, lambda s: send_direction(s).start())
            send_own(1).start()
            share.start()
            loop(2, nch, lambda s: send_own(s).start())
        one_block(chip, *stacked(chip), core, part)
        if part == 0:
            share.wait_recv()
            pbuf[other] = stack_points(pshare[other, :width, :])
        one_block(chip, *stacked(chip), other, part)

        def both(q, part=part):
            if part == 0:
                wait_direction(q)
            terms, weights = stacked(q)
            one_block(q, terms, weights, 0, part)
            one_block(q, terms, weights, 1, part)

        def step(s, part=part):
            q = chip_from(s)
            if part == 0:
                wait_slot(q)
            both(q)

        loop(1, nch, step)

        ibuf[part, 0] = jnp.sum(inn[...], axis=1, keepdims=True)
        exchange(part).start()
        exchange(part).wait_recv()
        inner = []
        for half in range(2):
            sums = (ibuf[part, 0, half] + ibuf[part, 1, half]) * (1.0 / math.sqrt(nch * 2 * cen_dev))
            mask = pshare[half, width:width + 1, pl.ds(part * blk, blk)]
            inner.append(rows_of(16, [jnp.where(mask > 0.5, sums, 0.0)]))

        def product(q, part=part, inner=inner):
            term = 0.0
            for half in range(2):
                term = term + lax.dot_general(
                    inner[half], kbuf[q, half], (((1,), (1,)), ((), ())), preferred_element_type=F32)[:1]
            tbuf[q] = term if part == 0 else tbuf[q] + term

        def owner(s, part=part):
            product(chip_to(nch - s))
            if part == nblk - 1:
                send_term(nch - s).start()

        loop(1, nch, owner)
        product(chip)

    share.wait_send()
    loop(1, nch, lambda s: send_own(s).wait_send())
    loop(1, nch, lambda s: send_direction(s).wait_send())
    for part in range(nblk):
        exchange(part).wait_send()
    out[...] = tbuf[chip]

    def gather(s):
        q = chip_from(s)
        copy(tbuf.at[q], rbuf.at[q], ts.at[s], tr.at[q], peer(q)).wait()
        out[...] += rbuf[q]

    loop(1, nch, gather)
    out[...] = out[...] * (1.0 / math.sqrt(slots * nch * 2))


def body(n, points, centres, direction, counts):
    width, slots = points.shape
    cen_dev = centres.shape[1]
    nch = n // 2
    nblk = 1
    while nch * cen_dev * 2 * (slots // nblk) * 2 > KERN_BYTES:
        nblk *= 2
    blk = slots // nblk
    depth = 6 * width + 16
    hbm = pl.BlockSpec(memory_space=pltpu.HBM)
    sem = pltpu.SemaphoreType.DMA
    got = pl.pallas_call(
        functools.partial(kernel, nch, nblk),
        out_shape=jax.ShapeDtypeStruct((1, cen_dev), F32),
        in_specs=[hbm, hbm, hbm, hbm],
        out_specs=pl.BlockSpec(memory_space=pltpu.VMEM),
        scratch_shapes=[
            pltpu.VMEM((2, width + 8, slots), F32),
            pltpu.VMEM((nch, width, cen_dev), F32),
            pltpu.VMEM((nch, 1, cen_dev), F32),
            pltpu.SMEM((1,), jnp.int32),
            pltpu.VMEM((2, depth, slots), BF16),
            pltpu.VMEM((nch, 2, cen_dev, blk), BF16),
            pltpu.VMEM((2, 16, blk), F32),
            pltpu.VMEM((nblk, 2, 2, 1, blk), F32),
            pltpu.VMEM((nch, 1, cen_dev), F32),
            pltpu.VMEM((nch, 1, cen_dev), F32),
            sem((4,)), sem((2,)), sem((nch,)), sem((nch,)), sem((nch,)), sem((nch,)), sem((nblk,)), sem((nblk,)), sem((nch,)), sem((nch,)),
        ],
        compiler_params=pltpu.CompilerParams(
            collective_id=0, has_side_effects=True, vmem_limit_bytes=63 << 20),
        cost_estimate=pl.CostEstimate(
            flops=2 * slots * n * cen_dev * (depth + 2), bytes_accessed=4 * width * (slots + cen_dev),
            transcendentals=slots * n * cen_dev),
    )(points, centres, direction.reshape(1, cen_dev), counts)
    return got.reshape(cen_dev)


def solution(mesh):
    placed = (
        P(None, ("groups", "dp")),
        P(None, ("groups", "dp")),
        P(("groups", "dp")),
        P(("groups", "dp")),
    )
    return jax.shard_map(
        functools.partial(body, mesh.shape["dp"]), mesh=mesh, in_specs=placed,
        out_specs=P(("groups", "dp")), check_vma=False)
```
